256 devices in a mesh: blk: 32 (over x, z), head: 8 (over y, core).
Axes of the slice: x: 4, y: 4, z: 8, core: 2. Of those that a mesh axis runs over, the one named last changes fastest.
Arguments:
- queries: bfloat16 [8192, 3072], P('blk', 'head'), may hold values from -5 to 5
- keys: bfloat16 [8192, 3072], P('blk', 'head'), may hold values from -5 to 5
- values: bfloat16 [8192, 3072], P('blk', 'head'), may hold values from -5 to 5
- query_tangent: bfloat16 [8192, 3072], P('blk', 'head'), may hold values from -5 to 5
- key_tangent: bfloat16 [8192, 3072], P('blk', 'head'), may hold values from -5 to 5
- value_tangent: bfloat16 [8192, 3072], P('blk', 'head'), may hold values from -5 to 5
- tile_mask: int32 [24, 64, 64], P('head'), may hold values from 0 to 1, as said below
- block_frame: int32 [32], replicated, may hold values from 0 to 31, each once
- out_weight: bfloat16 [3072, 3072], P('head'), may hold values from -1.25 to 1.25
Outputs:
- attn_out: bfloat16 [8192, 3072], P(('blk', 'head'))
- tangent_out: bfloat16 [8192, 3072], P(('blk', 'head'))
The draws below stay inside these ranges and needn't reach their ends.
Inputs may be any that keep to these rules, and one draw needn't show every extreme that they name: tile_mask[h, a, a] is 1 for every head and tile. `block_frame`: each frame block is held by exactly one index of blk.
All inputs are finite; a program needn't handle non-finite values.
Results may differ from the reference program's by a relative error of at most 0.02.
Values may be sent and summed in bfloat16 or wider, within the bound.
No kernel may reach another device: no remote copies, remote signals or barrier semaphores. Data moves between devices by JAX's collectives and lax.ppermute only.
A program may use at most 128 MiB of HBM per device.

```python
import jax
import jax.numpy as jnp
from jax import lax

HEADS = 24
HEAD_DIM = 128
DM = 3072
TILE = 128
TOK_DEV = 256
TOKENS = 8192
N_BLK = 32
N_HEAD = 8


def draw_queries(key, part):
    key = jax.random.fold_in(key, 1)
    drawn = 1.25 * jax.random.normal(key, (TOKENS, HEADS * HEAD_DIM), jnp.float32)
    return jnp.clip(drawn, -5.0, 5.0).astype(jnp.bfloat16)


def draw_keys(key, part):
    key = jax.random.fold_in(key, 2)
    drawn = 1.2 * jax.random.normal(key, (TOKENS, HEADS * HEAD_DIM), jnp.float32)
    return jnp.clip(drawn, -5.0, 5.0).astype(jnp.bfloat16)


def draw_tile_mask(key, part):
    key = jax.random.fold_in(key, 3)
    first_key, second_key, third_key = jax.random.split(key, 3)
    tiles_dev = TOK_DEV // TILE
    tile_count = TOKENS // TILE
    frame_count = TOKENS // TOK_DEV
    density = jnp.repeat(jax.random.randint(first_key, (frame_count,), 1, 9), tiles_dev)
    foreground = jax.random.randint(second_key, (HEADS, tile_count), 0, 8) < density[None, :]
    extra = jax.random.randint(third_key, (HEADS, tile_count, tile_count), 0, 32) == 0
    diagonal = jnp.eye(tile_count, dtype=jnp.bool_)[None, :, :]
    linked = foreground[:, :, None] & foreground[:, None, :] | extra | diagonal
    return linked.astype(jnp.int32)


def level_of(key, extent, pieces, least, largest):
    gain, own = 1.0, jax.random.fold_in(key, 6)
    for axis_at, shards_of in pieces:
        steps = jnp.exp(jax.random.uniform(jax.random.fold_in(own, axis_at), (shards_of,), jnp.float32, least / len(pieces), largest / len(pieces)))
        gain = gain * jnp.repeat(steps, extent[axis_at] // shards_of).reshape([-1 if axis == axis_at else 1 for axis in range(len(extent))])
    return gain


def centred(stream_key, dims, width, limit, pieces=(), kind=jnp.bfloat16):
    result = width * jax.random.normal(stream_key, dims, jnp.float32)
    if pieces:
        result = result * level_of(stream_key, dims, pieces, -0.22, 0.18)
    return jnp.clip(result, -limit, limit).astype(kind)


def setup_inputs(seed: int = 0) -> dict:
    key_of = jax.random.split(jax.random.key(seed), 10)
    return {
        "queries": draw_queries(jax.random.fold_in(key_of[9], 71), 0),
        "keys": draw_keys(jax.random.fold_in(key_of[9], 71), 0),
        "values": centred(key_of[2], (TOKENS, HEADS * HEAD_DIM), 1.0, 5.0, ((0, 32), (1, 8))),
        "query_tangent": centred(key_of[3], (TOKENS, HEADS * HEAD_DIM), 1.0, 5.0, ((0, 32), (1, 8))),
        "key_tangent": centred(key_of[4], (TOKENS, HEADS * HEAD_DIM), 1.0, 5.0, ((0, 32), (1, 8))),
        "value_tangent": centred(key_of[5], (TOKENS, HEADS * HEAD_DIM), 1.0, 5.0, ((0, 32), (1, 8))),
        "tile_mask": draw_tile_mask(jax.random.fold_in(key_of[9], 71), 0),
        "block_frame": jax.random.permutation(key_of[7], N_BLK).astype(jnp.int32),
        "out_weight": centred(key_of[8], (HEADS * HEAD_DIM, DM), (HEADS * HEAD_DIM // 128) ** -0.5, 1.25, ((0, 8),)),
    }


VERY_LOW = -1e30


def frame_tiles(block_frame):
    tokens = jnp.arange(TOKENS, dtype=jnp.int32)
    owners = tokens // TOK_DEV
    return (block_frame[owners] * (TOK_DEV // TILE) + (tokens % TOK_DEV) // TILE).astype(jnp.int32)


def by_head(array):
    return array.astype(jnp.float32).reshape(TOKENS, HEADS, HEAD_DIM).transpose(1, 0, 2)


def product(left, right):
    return jnp.dot(left, right, preferred_element_type=jnp.float32, precision=lax.Precision.HIGHEST)


def reference(queries, keys, values, query_tangent, key_tangent, value_tangent, tile_mask, block_frame, out_weight):
    scaling = HEAD_DIM ** -0.5
    ftile = frame_tiles(block_frame)
    offsets = jnp.arange(TOKENS // TOK_DEV, dtype=jnp.int32) * TOK_DEV

    def one_head(packed):
        query_head, key_head, value_head, qtan_head, ktan_head, vtan_head, mask_head = packed
        key_columns = mask_head[:, ftile]

        def one_block(offset):
            query_rows = lax.dynamic_slice_in_dim(query_head, offset, TOK_DEV, 0)
            qtan_rows = lax.dynamic_slice_in_dim(qtan_head, offset, TOK_DEV, 0)
            row_tiles = lax.dynamic_slice_in_dim(ftile, offset, TOK_DEV, 0)
            is_live = key_columns[row_tiles] == 1
            scores = scaling * product(query_rows, key_head.T)
            tangent_scores = scaling * (product(qtan_rows, key_head.T) + product(query_rows, ktan_head.T))
            row_max = jnp.max(jnp.where(is_live, scores, VERY_LOW), axis=1, keepdims=True)
            weights = jnp.where(is_live, jnp.exp(scores - row_max), 0.0)
            totals = jnp.sum(weights, axis=1, keepdims=True)
            scaled = weights * tangent_scores
            drifts = jnp.sum(scaled, axis=1, keepdims=True)
            weights_b = lax.optimization_barrier(weights.astype(jnp.bfloat16)).astype(jnp.float32)
            scaled_b = lax.optimization_barrier(scaled.astype(jnp.bfloat16)).astype(jnp.float32)
            attn = product(weights_b, value_head) / totals
            attn_tangent = (product(scaled_b, value_head) + product(weights_b, vtan_head)) / totals - (drifts / totals) * attn
            return attn.astype(jnp.bfloat16), attn_tangent.astype(jnp.bfloat16)

        mixed_head, tangent_head = lax.map(one_block, offsets)
        return mixed_head.reshape(TOKENS, HEAD_DIM), tangent_head.reshape(TOKENS, HEAD_DIM)

    mixed, mixed_tangent = lax.map(one_head, (by_head(queries), by_head(keys), by_head(values), by_head(query_tangent), by_head(key_tangent), by_head(value_tangent), tile_mask))
    mixed = mixed.transpose(1, 0, 2).reshape(TOKENS, HEADS * HEAD_DIM).astype(jnp.float32)
    mixed_tangent = mixed_tangent.transpose(1, 0, 2).reshape(TOKENS, HEADS * HEAD_DIM).astype(jnp.float32)
    weight_full = out_weight.astype(jnp.float32)
    group_width = (HEADS // N_HEAD) * HEAD_DIM
    attn_out = jnp.zeros((TOKENS, DM), jnp.float32)
    tangent_out = jnp.zeros((TOKENS, DM), jnp.float32)
    for group_index in range(N_HEAD):
        low_col = group_index * group_width
        weight_rows = weight_full[low_col:low_col + group_width]
        partial_main = product(mixed[:, low_col:low_col + group_width], weight_rows)
        partial_tan = product(mixed_tangent[:, low_col:low_col + group_width], weight_rows)
        attn_out = attn_out + lax.optimization_barrier(partial_main.astype(jnp.bfloat16)).astype(jnp.float32)
        tangent_out = tangent_out + lax.optimization_barrier(partial_tan.astype(jnp.bfloat16)).astype(jnp.float32)
    return attn_out.astype(jnp.bfloat16), tangent_out.astype(jnp.bfloat16)
```

```python
import functools
import math

import jax
import jax.numpy as jnp
from jax import lax
from jax.experimental import pallas as pl
from jax.experimental.pallas import tpu as pltpu
from jax.sharding import Mesh
from jax.sharding import PartitionSpec as P

NX, NZ, NY, NC = 4, 8, 4, 2
HEADS_HERE = 3
HEAD_DIM = 128
PAIR = 2 * HEAD_DIM
TILE = 128
TOK = 256
TILES_HERE = TOK // TILE
FRAME_TILES = NX * NZ * TILES_HERE
WIDE = HEADS_HERE * PAIR
PACKED = WIDE + 128
PIECES = 3
SLOT_TOK = TOK // NY
DM = 3072
SCALING = HEAD_DIM ** (-0.5)
EXP_SCALE = SCALING * math.log2(math.e)
VERY_LOW = -1e30
VERY_HIGH = 1e30
VMEM_LIMIT = 56 * 1024 * 1024
NT = (((1,), (1,)), ((), ()))


def params():
    return pltpu.CompilerParams(vmem_limit_bytes=VMEM_LIMIT)


def prepare_kernel(q_ref, qt_ref, k_ref, kt_ref, v_ref, vt_ref, qq_ref, kv_ref):
    for h in range(HEADS_HERE):
        cols = pl.ds(h * HEAD_DIM, HEAD_DIM)
        qq_ref[:, pl.ds(h * PAIR, HEAD_DIM)] = qt_ref[:, cols]
        qq_ref[:, pl.ds(h * PAIR + HEAD_DIM, HEAD_DIM)] = q_ref[:, cols]
        kv_ref[h, :, 0:HEAD_DIM] = k_ref[:, cols]
        kv_ref[h, :, HEAD_DIM:PAIR] = kt_ref[:, cols]
        kv_ref[HEADS_HERE + h, 0:HEAD_DIM, :] = v_ref[:, cols].T
        kv_ref[HEADS_HERE + h, HEAD_DIM:PAIR, :] = vt_ref[:, cols].T


def prepare(queries, query_tangent, keys, key_tangent, values, value_tangent):
    return pl.pallas_call(
        prepare_kernel,
        out_shape=(
            jax.ShapeDtypeStruct((TOK, WIDE), jnp.bfloat16),
            jax.ShapeDtypeStruct((2 * HEADS_HERE, TOK, PAIR), jnp.bfloat16),
        ),
        compiler_params=params(),
        name="prepare",
    )(queries, query_tangent, keys, key_tangent, values, value_tangent)


def attend_slot(h, slot, key_blocks, q2, mask_ref, frame_ref, place_ref, kks, vvs, old):
    x, z = place_ref[0], place_ref[1]
    query_frame = frame_ref[((x + slot) % NX) * NZ + z]
    lanes = lax.broadcasted_iota(jnp.int32, (1, TOK), 1)
    first = lanes < TILE
    m_old, l_old, d_old, acc_old = old
    scores, lives = [], []
    m_new = m_old
    for at, offset in enumerate(key_blocks):
        key_frame = frame_ref[x * NZ + (z + offset + NZ) % NZ]
        s = lax.dot_general(
            kks[at][:, 0:HEAD_DIM], q2[:, HEAD_DIM:PAIR], NT, preferred_element_type=jnp.float32
        )
        for j in range(TILES_HERE):
            row = (h * FRAME_TILES + query_frame * TILES_HERE) * FRAME_TILES
            col = key_frame * TILES_HERE + j
            live = jnp.where(first, mask_ref[row + col], mask_ref[row + FRAME_TILES + col]) == 1
            s_tile = s[j * TILE : (j + 1) * TILE]
            top = jnp.max(s_tile, axis=0, keepdims=True) * EXP_SCALE
            m_new = jnp.maximum(m_new, jnp.where(live, top, VERY_LOW))
            scores.append(s_tile)
            lives.append(live)
    fade = jnp.exp2(m_old - m_new)
    l_new, d_sum = l_old * fade, jnp.zeros_like(d_old)
    main, side = None, None
    for at in range(len(key_blocks)):
        t = lax.dot_general(kks[at][...], q2, NT, preferred_element_type=jnp.float32)
        weights, scaled = [], []
        for j in range(TILES_HERE):
            less = jnp.where(lives[TILES_HERE * at + j], m_new, VERY_HIGH)
            w = jnp.exp2(scores[TILES_HERE * at + j] * EXP_SCALE - less)
            ws = w * t[j * TILE : (j + 1) * TILE]
            l_new = l_new + jnp.sum(w, axis=0, keepdims=True)
            d_sum = d_sum + jnp.sum(ws, axis=0, keepdims=True)
            weights.append(w.astype(jnp.bfloat16))
            scaled.append(ws.astype(jnp.bfloat16))
        weights = jnp.concatenate(weights, axis=0)
        scaled = jnp.concatenate(scaled, axis=0)
        o = jnp.dot(vvs[at][...], weights, preferred_element_type=jnp.float32)
        o2 = jnp.dot(vvs[at][0:HEAD_DIM, :], scaled, preferred_element_type=jnp.float32)
        main = o if main is None else main + o
        side = o2 if side is None else side + o2
    d_new = d_old * fade + SCALING * d_sum
    top = acc_old[0:HEAD_DIM] * fade + main[0:HEAD_DIM]
    bottom = acc_old[HEAD_DIM:PAIR] * fade + main[HEAD_DIM:PAIR] + SCALING * side
    return m_new, l_new, d_new, top, bottom


def attend_kernel(key_blocks, is_first, is_last, *refs):
    count = len(key_blocks)
    mask_ref, frame_ref, place_ref = refs[:3]
    q_refs = refs[3 : 3 + NX]
    rest = refs[3 + NX :]
    kk_refs = [r.at[0] for r in rest[:count]]
    vv_refs = [r.at[0] for r in rest[count : 2 * count]]
    rest = rest[2 * count :]
    if not is_first:
        acc_in, stat_in = rest[:2]
        rest = rest[2:]
    h = pl.program_id(0)
    if is_last:
        side_ref = rest[1]

        @pl.when(h == 0)
        def _():
            side_ref[...] = jnp.zeros_like(side_ref)

    for slot in range(NX):
        cols = pl.ds(slot * TOK, TOK)
        if is_first:
            zero = jnp.zeros((1, TOK), jnp.float32)
            old = (zero + VERY_LOW, zero, zero, jnp.zeros((PAIR, TOK), jnp.float32))
        else:
            old = (
                stat_in[0, 0:1, cols],
                stat_in[0, 1:2, cols],
                stat_in[0, 2:3, cols],
                acc_in[0, :, cols],
            )
        m, l, d, top, bottom = attend_slot(
            h, slot, key_blocks, q_refs[slot][...], mask_ref, frame_ref, place_ref, kk_refs, vv_refs, old
        )
        if not is_last:
            acc_out, stat_out = rest
            stat_out[0, 0:1, cols] = m
            stat_out[0, 1:2, cols] = l
            stat_out[0, 2:3, cols] = d
            acc_out[0, 0:HEAD_DIM, cols] = top
            acc_out[0, HEAD_DIM:PAIR, cols] = bottom
        else:
            out_ref = rest[0]
            some = l > 0.0
            inverse = jnp.where(some, 1.0 / jnp.where(some, l, 1.0), 0.0)
            level = jnp.where(some, m + jnp.log2(jnp.where(some, l, 1.0)), VERY_LOW)
            drift = d * inverse
            attn = top * inverse
            tangent = bottom * inverse - drift * attn
            target = (place_ref[0] + slot) % NX
            columns = pl.multiple_of(h * PAIR, PAIR)
            out_ref[target, :, pl.ds(columns, HEAD_DIM)] = attn.astype(jnp.bfloat16).T
            out_ref[target, :, pl.ds(columns + HEAD_DIM, HEAD_DIM)] = tangent.astype(jnp.bfloat16).T
            for at, value in enumerate((level, drift)):
                left = value
                for p in range(PIECES):
                    piece = left.astype(jnp.bfloat16).astype(jnp.float32)
                    side_ref[slot, pl.ds(8 * p + HEADS_HERE * at + h, 1), :] = piece
                    left = left - piece

            @pl.when(h == HEADS_HERE - 1)
            def _():
                out_ref[target, :, pl.ds(WIDE, 128)] = side_ref[slot].T.astype(jnp.bfloat16)


def attend(key_blocks, mask, frames, place, slots, kks, vvs, state, is_last):
    count = len(key_blocks)
    is_first = state is None
    smem = pl.BlockSpec(memory_space=pltpu.SMEM)
    acc_spec = pl.BlockSpec((1, PAIR, NX * TOK), lambda h: (h, 0, 0))
    stat_spec = pl.BlockSpec((1, 8, NX * TOK), lambda h: (h, 0, 0))
    in_specs = [smem] * 3
    in_specs += [pl.BlockSpec((TOK, PAIR), lambda h: (0, h))] * NX
    in_specs += [pl.BlockSpec((1, TOK, PAIR), lambda h: (h, 0, 0))] * count
    for vv in vvs:
        skip = vv.shape[0] - HEADS_HERE
        in_specs.append(pl.BlockSpec((1, PAIR, TOK), lambda h, skip=skip: (skip + h, 0, 0)))
    operands = [mask, frames, place, *slots, *kks, *vvs]
    if not is_first:
        in_specs += [acc_spec, stat_spec]
        operands += list(state)
    scratch = []
    if is_last:
        out_shape = jax.ShapeDtypeStruct((NX, TOK, PACKED), jnp.bfloat16)
        out_specs = pl.BlockSpec((NX, TOK, PACKED), lambda h: (0, 0, 0))
        scratch = [pltpu.VMEM((NX, 128, TOK), jnp.float32)]
    else:
        out_shape = (
            jax.ShapeDtypeStruct((HEADS_HERE, PAIR, NX * TOK), jnp.float32),
            jax.ShapeDtypeStruct((HEADS_HERE, 8, NX * TOK), jnp.float32),
        )
        out_specs = (acc_spec, stat_spec)
    return pl.pallas_call(
        functools.partial(attend_kernel, key_blocks, is_first, is_last),
        grid=(HEADS_HERE,),
        in_specs=in_specs,
        out_specs=out_specs,
        out_shape=out_shape,
        scratch_shapes=scratch,
        compiler_params=params(),
        name="attend_last" if is_last else "attend",
    )(*operands)


COLS = 512


def project_kernel(place_ref, r_ref, w_ref, main_ref, tangent_ref, other_ref, mixed):
    c = place_ref[3]

    @pl.when(pl.program_id(0) == 0)
    def _():
        for group in range(NY):
            sides = []
            for x in range(NX):
                side = r_ref[x * NY + group, :, pl.ds(WIDE, 128)].astype(jnp.float32)
                sides.append(side + (pltpu.roll(side, 128 - 8, 1) + pltpu.roll(side, 128 - 16, 1)))
            top = functools.reduce(jnp.maximum, sides)
            shares = [jnp.exp2(side - top) for side in sides]
            inverse = 1.0 / sum(shares)
            shares = [share * inverse for share in shares]
            drifts = [pltpu.roll(side, 128 - HEADS_HERE, 1) for side in sides]
            drift = sum(s * d for s, d in zip(shares, drifts))
            moves = [s * (d - drift) for s, d in zip(shares, drifts)]
            for h in range(HEADS_HERE):
                attn, tangent = 0.0, 0.0
                for x in range(NX):
                    a = r_ref[x * NY + group, :, pl.ds(h * PAIR, HEAD_DIM)].astype(jnp.float32)
                    t = r_ref[x * NY + group, :, pl.ds(h * PAIR + HEAD_DIM, HEAD_DIM)].astype(jnp.float32)
                    share = shares[x][:, h : h + 1]
                    attn = attn + share * a
                    tangent = tangent + share * t + moves[x][:, h : h + 1] * a
                cols = pl.ds((group * HEADS_HERE + h) * HEAD_DIM, HEAD_DIM)
                mixed[0:SLOT_TOK, cols] = attn.astype(jnp.bfloat16)
                mixed[SLOT_TOK : 2 * SLOT_TOK, cols] = tangent.astype(jnp.bfloat16)

    total = jnp.dot(mixed[...], w_ref[...], preferred_element_type=jnp.float32)
    half = SLOT_TOK // NC
    mine = c == 0
    for which, own_ref in enumerate((main_ref, tangent_ref)):
        low = total[which * SLOT_TOK : which * SLOT_TOK + half]
        high = total[which * SLOT_TOK + half : (which + 1) * SLOT_TOK]
        own_ref[...] = jnp.where(mine, low, high)
        other_ref[which] = jnp.where(mine, high, low).astype(jnp.bfloat16)


def project(place, received, weight):
    half = SLOT_TOK // NC
    rows = NY * HEADS_HERE * HEAD_DIM
    own_spec = pl.BlockSpec((half, COLS), lambda i: (0, i))
    own_shape = jax.ShapeDtypeStruct((half, DM), jnp.float32)
    return pl.pallas_call(
        project_kernel,
        grid=(DM // COLS,),
        in_specs=[
            pl.BlockSpec(memory_space=pltpu.SMEM),
            pl.BlockSpec((NX * NY, SLOT_TOK, PACKED), lambda i: (0, 0, 0)),
            pl.BlockSpec((rows, COLS), lambda i: (0, i)),
        ],
        out_specs=(own_spec, own_spec, pl.BlockSpec((2, half, COLS), lambda i: (0, 0, i))),
        out_shape=(own_shape, own_shape, jax.ShapeDtypeStruct((2, half, DM), jnp.bfloat16)),
        scratch_shapes=[pltpu.VMEM((2 * SLOT_TOK, rows), jnp.bfloat16)],
        compiler_params=params(),
        name="project",
    )(place, received, weight)


def finish_kernel(main_ref, tangent_ref, arrived_ref, out_ref, tout_ref):
    out_ref[...] = (main_ref[...] + arrived_ref[0].astype(jnp.float32)).astype(jnp.bfloat16)
    tout_ref[...] = (tangent_ref[...] + arrived_ref[1].astype(jnp.float32)).astype(jnp.bfloat16)


def finish(main, tangent, arrived):
    shape = jax.ShapeDtypeStruct(main.shape, jnp.bfloat16)
    return pl.pallas_call(
        finish_kernel, out_shape=(shape, shape), compiler_params=params(), name="finish"
    )(main, tangent, arrived)


def shifted(block, axis, distance):
    size = lax.axis_size(axis)
    return lax.ppermute(block, axis, [(i, (i + distance) % size) for i in range(size)])


def body(
    queries,
    keys,
    values,
    query_tangent,
    key_tangent,
    value_tangent,
    tile_mask,
    block_frame,
    out_weight,
):
    place = jnp.stack([lax.axis_index(a) for a in ("x", "z", "y", "c")]).astype(jnp.int32)
    mask = tile_mask.reshape(-1)
    qq, bundle = prepare(queries, query_tangent, keys, key_tangent, values, value_tangent)

    weight = lax.all_gather(out_weight, "y", tiled=True)

    slots = [qq, shifted(qq, "x", -1), shifted(qq, "x", 2), shifted(qq, "x", 1)]
    from_left = shifted(bundle, "z", 1)
    from_right = shifted(bundle, "z", -1)
    from_left, from_right, slots, mask = lax.optimization_barrier(
        (from_left, from_right, slots, mask)
    )

    def run(key_blocks, kks, vvs, state, is_last=False):
        return attend(key_blocks, mask, block_frame, place, slots, kks, vvs, state, is_last)

    blocks = (bundle, from_left, from_right)
    offsets = (0, -1, 1)
    state = None
    for distance in (2, 3):
        next_left = shifted(from_left, "z", 1)
        next_right = shifted(from_right, "z", -1)
        state = run(offsets, blocks, blocks, state)
        from_left, from_right, state = lax.optimization_barrier((next_left, next_right, state))
        blocks = (from_left, from_right)
        offsets = (-distance, distance)
    far_keys = shifted(from_left[:HEADS_HERE], "z", 1)
    far_values = shifted(from_right[HEADS_HERE:], "z", -1)
    state = run(offsets, blocks, blocks, state)
    far_keys, far_values, state = lax.optimization_barrier((far_keys, far_values, state))
    packed = run((4,), (far_keys,), (far_values,), state, is_last=True)
    received = lax.all_to_all(
        packed.reshape(NX * NY, SLOT_TOK, PACKED), ("x", "y"), 0, 0, tiled=True
    )
    main, tangent, other = project(place, received, weight)
    arrived = lax.ppermute(other, "c", [(0, 1), (1, 0)])
    return finish(main, tangent, arrived)


def solution(mesh):
    inner = Mesh(mesh.devices.reshape(NX, NZ, NY, NC), ("x", "z", "y", "c"))
    blk, head = ("x", "z"), ("y", "c")
    in_specs = (
        P(blk, head),
        P(blk, head),
        P(blk, head),
        P(blk, head),
        P(blk, head),
        P(blk, head),
        P(head, None, None),
        P(),
        P(head, None),
    )
    out_specs = (P(blk + head, None), P(blk + head, None))
    return jax.shard_map(body, mesh=inner, in_specs=in_specs, out_specs=out_specs, check_vma=False)
```

```python
import functools
import math

import jax
import jax.numpy as jnp
from jax import lax
from jax.experimental import pallas as pl
from jax.experimental.pallas import tpu as pltpu
from jax.sharding import Mesh
from jax.sharding import PartitionSpec as P

NX, NZ, NY, NC = 4, 8, 4, 2
HEADS_HERE = 3
HEAD_DIM = 128
PAIR = 2 * HEAD_DIM
TILE = 128
TOK = 256
TILES_HERE = TOK // TILE
FRAME_TILES = NX * NZ * TILES_HERE
WIDE = HEADS_HERE * PAIR
PACKED = WIDE + 128
PIECES = 3
WITH_ONES = HEAD_DIM + 16
SLOT_TOK = TOK // NY
DM = 3072
SCALING = HEAD_DIM ** (-0.5)
EXP_SCALE = SCALING * math.log2(math.e)
VERY_LOW = -1e30
VERY_HIGH = 1e30
VMEM_LIMIT = 56 * 1024 * 1024
NT = (((1,), (1,)), ((), ()))


def params():
    return pltpu.CompilerParams(vmem_limit_bytes=VMEM_LIMIT)


def prepare_kernel(q_ref, qt_ref, k_ref, kt_ref, v_ref, vt_ref, qq_ref, kv_ref):
    for h in range(HEADS_HERE):
        cols = pl.ds(h * HEAD_DIM, HEAD_DIM)
        qq_ref[:, pl.ds(h * PAIR, HEAD_DIM)] = qt_ref[:, cols]
        qq_ref[:, pl.ds(h * PAIR + HEAD_DIM, HEAD_DIM)] = q_ref[:, cols]
        kv_ref[h, :, 0:HEAD_DIM] = k_ref[:, cols]
        kv_ref[h, :, HEAD_DIM:PAIR] = kt_ref[:, cols]
        kv_ref[HEADS_HERE + h, 0:HEAD_DIM, :] = v_ref[:, cols].T
        kv_ref[HEADS_HERE + h, HEAD_DIM:PAIR, :] = vt_ref[:, cols].T


def prepare(queries, query_tangent, keys, key_tangent, values, value_tangent):
    return pl.pallas_call(
        prepare_kernel,
        out_shape=(
            jax.ShapeDtypeStruct((TOK, WIDE), jnp.bfloat16),
            jax.ShapeDtypeStruct((2 * HEADS_HERE, TOK, PAIR), jnp.bfloat16),
        ),
        compiler_params=params(),
        name="prepare",
    )(queries, query_tangent, keys, key_tangent, values, value_tangent)


def turned(array):
    size = array.shape[1]
    row = lax.broadcasted_iota(jnp.int32, (size, size), 0)
    col = lax.broadcasted_iota(jnp.int32, (size, size), 1)
    identity = jnp.where(row == col, 1.0, 0.0).astype(jnp.bfloat16)
    return lax.dot_general(identity, array, NT, preferred_element_type=jnp.float32).astype(jnp.bfloat16)


def products(kk, q2):
    s = lax.dot_general(
        kk[:, 0:HEAD_DIM], q2[:, HEAD_DIM:PAIR], NT, preferred_element_type=jnp.float32
    )
    return s, lax.dot_general(kk, q2, NT, preferred_element_type=jnp.float32)


def attend_slot(h, slot, key_blocks, s, t, mask_ref, frame_ref, place_ref, vv_ref, old):
    x, z = place_ref[0], place_ref[1]
    query_frame = frame_ref[((x + slot) & (NX - 1)) * NZ + z]
    lanes = lax.broadcasted_iota(jnp.int32, (1, TOK), 1)
    first = lanes < TILE
    m_old, l_old, d_old, acc_old = old
    lives = []
    m_new = m_old
    for at, offset in enumerate(key_blocks):
        key_frame = frame_ref[x * NZ + ((z + offset) & (NZ - 1))]
        for j in range(TILES_HERE):
            row = (h * FRAME_TILES + query_frame * TILES_HERE) * FRAME_TILES
            col = key_frame * TILES_HERE + j
            live = jnp.where(first, mask_ref[row + col], mask_ref[row + FRAME_TILES + col]) == 1
            tile = at * TILES_HERE + j
            top = jnp.max(s[tile * TILE : (tile + 1) * TILE], axis=0, keepdims=True) * EXP_SCALE
            m_new = jnp.maximum(m_new, jnp.where(live, top, VERY_LOW))
            lives.append(live)
    fade = jnp.exp2(m_old - m_new)
    weights, scaled = [], []
    for tile, live in enumerate(lives):
        rows = slice(tile * TILE, (tile + 1) * TILE)
        w = jnp.exp2(s[rows] * EXP_SCALE - jnp.where(live, m_new, VERY_HIGH))
        weights.append(w.astype(jnp.bfloat16))
        scaled.append((w * t[rows]).astype(jnp.bfloat16))
    o = jnp.dot(vv_ref[...], jnp.concatenate(weights, axis=0), preferred_element_type=jnp.float32)
    o2 = jnp.dot(
        vv_ref[0:WITH_ONES, :], jnp.concatenate(scaled, axis=0), preferred_element_type=jnp.float32
    )
    l_new = l_old * fade + o[HEAD_DIM : HEAD_DIM + 1]
    d_new = d_old * fade + SCALING * o2[HEAD_DIM : HEAD_DIM + 1]
    top = acc_old[0:HEAD_DIM] * fade + o[0:HEAD_DIM]
    bottom = acc_old[HEAD_DIM:PAIR] * fade + (o[WITH_ONES:] + SCALING * o2[0:HEAD_DIM])
    return m_new, l_new, d_new, top, bottom


def attend_kernel(key_blocks, is_first, is_last, *refs):
    count = len(key_blocks)
    mask_ref, frame_ref, place_ref = refs[:3]
    q_refs = refs[3 : 3 + NX]
    rest = refs[3 + NX :]
    kk_refs = [r.at[0] for r in rest[:count]]
    vv_refs = [r.at[0] for r in rest[count : 2 * count]]
    rest = rest[2 * count :]
    if not is_first:
        acc_in, stat_in = rest[:2]
        rest = rest[2:]
    rest, vv_ref = rest[:-1], rest[-1]
    h = pl.program_id(0)
    kk = jnp.concatenate([r[...] for r in kk_refs], axis=0)
    for at in range(count):
        cols = pl.ds(at * TOK, TOK)
        vv_ref[0:HEAD_DIM, cols] = vv_refs[at][0:HEAD_DIM, :]
        vv_ref[HEAD_DIM:WITH_ONES, cols] = jnp.ones((WITH_ONES - HEAD_DIM, TOK), jnp.bfloat16)
        vv_ref[WITH_ONES:, cols] = vv_refs[at][HEAD_DIM:PAIR, :]
    if is_last:
        side_ref = rest[1]

        @pl.when(h == 0)
        def _():
            side_ref[...] = jnp.zeros_like(side_ref)

    ahead = [products(kk, q_refs[slot][...]) for slot in range(NX)]
    for slot in range(NX):
        cols = pl.ds(slot * TOK, TOK)
        if is_first:
            zero = jnp.zeros((1, TOK), jnp.float32)
            old = (zero + VERY_LOW, zero, zero, jnp.zeros((PAIR, TOK), jnp.float32))
        else:
            old = (
                stat_in[0, 0:1, cols],
                stat_in[0, 1:2, cols],
                stat_in[0, 2:3, cols],
                acc_in[0, :, cols],
            )
        m, l, d, top, bottom = attend_slot(
            h, slot, key_blocks, *ahead[slot], mask_ref, frame_ref, place_ref, vv_ref, old
        )
        if not is_last:
            acc_out, stat_out = rest
            stat_out[0, 0:1, cols] = m
            stat_out[0, 1:2, cols] = l
            stat_out[0, 2:3, cols] = d
            acc_out[0, 0:HEAD_DIM, cols] = top
            acc_out[0, HEAD_DIM:PAIR, cols] = bottom
        else:
            out_ref = rest[0]
            some = l > 0.0
            inverse = jnp.where(some, 1.0 / jnp.where(some, l, 1.0), 0.0)
            level = jnp.where(some, m + jnp.log2(jnp.where(some, l, 1.0)), VERY_LOW)
            drift = d * inverse
            attn = top * inverse
            tangent = bottom * inverse - drift * attn
            target = (place_ref[0] + slot) & (NX - 1)
            columns = pl.multiple_of(h * PAIR, PAIR)
            both = jnp.concatenate((attn, tangent), axis=0).astype(jnp.bfloat16)
            out_ref[target, :, pl.ds(columns, PAIR)] = both.T
            for at, value in enumerate((level, drift)):
                left = value
                for p in range(PIECES):
                    piece = left.astype(jnp.bfloat16).astype(jnp.float32)
                    side_ref[slot, pl.ds(8 * p + HEADS_HERE * at + h, 1), :] = piece
                    left = left - piece

    if is_last:

        @pl.when(h == HEADS_HERE - 1)
        def _():
            for slot in range(NX):
                target = (place_ref[0] + slot) & (NX - 1)
                out_ref[target, :, pl.ds(WIDE, 128)] = side_ref[slot].astype(jnp.bfloat16).T


def attend(key_blocks, mask, frames, place, slots, kks, vvs, state, is_last):
    count = len(key_blocks)
    is_first = state is None
    smem = pl.BlockSpec(memory_space=pltpu.SMEM)
    acc_spec = pl.BlockSpec((1, PAIR, NX * TOK), lambda h: (h, 0, 0))
    stat_spec = pl.BlockSpec((1, 8, NX * TOK), lambda h: (h, 0, 0))
    in_specs = [smem] * 3
    in_specs += [pl.BlockSpec((TOK, PAIR), lambda h: (0, h))] * NX
    in_specs += [pl.BlockSpec((1, TOK, PAIR), lambda h: (h, 0, 0))] * count
    for vv in vvs:
        skip = vv.shape[0] - HEADS_HERE
        in_specs.append(pl.BlockSpec((1, PAIR, TOK), lambda h, skip=skip: (skip + h, 0, 0)))
    operands = [mask, frames, place, *slots, *kks, *vvs]
    if not is_first:
        in_specs += [acc_spec, stat_spec]
        operands += list(state)
    scratch = [pltpu.VMEM((WITH_ONES + HEAD_DIM, count * TOK), jnp.bfloat16)]
    if is_last:
        out_shape = jax.ShapeDtypeStruct((NX, TOK, PACKED), jnp.bfloat16)
        out_specs = pl.BlockSpec((NX, TOK, PACKED), lambda h: (0, 0, 0))
        scratch = [pltpu.VMEM((NX, 128, TOK), jnp.float32)] + scratch
    else:
        out_shape = (
            jax.ShapeDtypeStruct((HEADS_HERE, PAIR, NX * TOK), jnp.float32),
            jax.ShapeDtypeStruct((HEADS_HERE, 8, NX * TOK), jnp.float32),
        )
        out_specs = (acc_spec, stat_spec)
    return pl.pallas_call(
        functools.partial(attend_kernel, key_blocks, is_first, is_last),
        grid=(HEADS_HERE,),
        in_specs=in_specs,
        out_specs=out_specs,
        out_shape=out_shape,
        scratch_shapes=scratch,
        compiler_params=params(),
        cost_estimate=pl.CostEstimate(
            flops=count * NX * HEADS_HERE * 12 * TOK * TOK * HEAD_DIM,
            transcendentals=count * NX * HEADS_HERE * TOK * TOK,
            bytes_accessed=8 * 1024 * 1024,
        ),
        name="attend_last" if is_last else "attend",
    )(*operands)


COLS = 512


def project_kernel(place_ref, *refs):
    sources, (main_ref, tangent_ref, other_ref, mixed, r_ref) = refs[:6], refs[6:11]
    targets, sems = (r_ref,) + refs[11:16], refs[16]
    copies = [
        pltpu.make_async_copy(source, target, sems.at[i])
        for i, (source, target) in enumerate(zip(sources, targets))
    ]
    for copy in copies:
        copy.start()
    y, c = place_ref[2], place_ref[3]
    copies[0].wait()
    for rel, shift in enumerate((0, NY - 1, 1, 2)):
        group = (y + shift) & (NY - 1)
        sides = []
        for x in range(NX):
            side = r_ref[x * NY + group, :, pl.ds(WIDE, 128)].astype(jnp.float32)
            sides.append(side + (pltpu.roll(side, 128 - 8, 1) + pltpu.roll(side, 128 - 16, 1)))
        top = functools.reduce(jnp.maximum, sides)
        shares = [jnp.exp2(side - top) for side in sides]
        inverse = 1.0 / sum(shares)
        shares = [share * inverse for share in shares]
        drifts = [pltpu.roll(side, 128 - HEADS_HERE, 1) for side in sides]
        drift = sum(s * d for s, d in zip(shares, drifts))
        moves = [s * (d - drift) for s, d in zip(shares, drifts)]
        for h in range(HEADS_HERE):
            attn, tangent = 0.0, 0.0
            for x in range(NX):
                a = r_ref[x * NY + group, :, pl.ds(h * PAIR, HEAD_DIM)].astype(jnp.float32)
                t = r_ref[x * NY + group, :, pl.ds(h * PAIR + HEAD_DIM, HEAD_DIM)].astype(jnp.float32)
                share = shares[x][:, h : h + 1]
                attn = attn + share * a
                tangent = tangent + share * t + moves[x][:, h : h + 1] * a
            cols = pl.ds((rel * HEADS_HERE + h) * HEAD_DIM, HEAD_DIM)
            mixed[0:SLOT_TOK, cols] = attn.astype(jnp.bfloat16)
            mixed[SLOT_TOK : 2 * SLOT_TOK, cols] = tangent.astype(jnp.bfloat16)

    for copy in copies[1:]:
        copy.wait()
    half = SLOT_TOK // NC
    mine = c == 0
    for column in range(0, DM, COLS):
        cols = pl.ds(column, COLS)
        total, start = 0.0, 0
        for ref in targets[1:]:
            rows = pl.ds(start, ref.shape[0])
            start += ref.shape[0]
            total = total + jnp.dot(mixed[:, rows], ref[:, cols], preferred_element_type=jnp.float32)
        for which, own_ref in enumerate((main_ref, tangent_ref)):
            low = total[which * SLOT_TOK : which * SLOT_TOK + half]
            high = total[which * SLOT_TOK + half : (which + 1) * SLOT_TOK]
            own_ref[:, cols] = jnp.where(mine, low, high)
            other_ref[which, :, cols] = jnp.where(mine, high, low).astype(jnp.bfloat16)


def project(place, received, weights):
    half = SLOT_TOK // NC
    own_shape = jax.ShapeDtypeStruct((half, DM), jnp.float32)
    anywhere = pl.BlockSpec(memory_space=pltpu.HBM)
    operands = (received, *weights)
    return pl.pallas_call(
        project_kernel,
        in_specs=[pl.BlockSpec(memory_space=pltpu.SMEM)] + [anywhere] * len(operands),
        out_shape=(own_shape, own_shape, jax.ShapeDtypeStruct((2, half, DM), jnp.bfloat16)),
        scratch_shapes=[
            pltpu.VMEM((2 * SLOT_TOK, NY * HEADS_HERE * HEAD_DIM), jnp.bfloat16),
            *[pltpu.VMEM(operand.shape, operand.dtype) for operand in operands],
            pltpu.SemaphoreType.DMA((len(operands),)),
        ],
        compiler_params=params(),
        name="project",
    )(place, *operands)


def finish_kernel(main_ref, tangent_ref, arrived_ref, out_ref, tout_ref):
    out_ref[...] = (main_ref[...] + arrived_ref[0].astype(jnp.float32)).astype(jnp.bfloat16)
    tout_ref[...] = (tangent_ref[...] + arrived_ref[1].astype(jnp.float32)).astype(jnp.bfloat16)


def finish(main, tangent, arrived):
    shape = jax.ShapeDtypeStruct(main.shape, jnp.bfloat16)
    return pl.pallas_call(
        finish_kernel, out_shape=(shape, shape), compiler_params=params(), name="finish"
    )(main, tangent, arrived)


def shifted(block, axis, distance):
    size = lax.axis_size(axis)
    return lax.ppermute(block, axis, [(i, (i + distance) % size) for i in range(size)])


def after(array, *others):
    return lax.optimization_barrier((array, *others))[0]


def body(
    queries,
    keys,
    values,
    query_tangent,
    key_tangent,
    value_tangent,
    tile_mask,
    block_frame,
    out_weight,
):
    place = jnp.stack([lax.axis_index(a) for a in ("x", "z", "y", "c")]).astype(jnp.int32)
    mask = tile_mask.reshape(-1)
    qq, bundle = prepare(queries, query_tangent, keys, key_tangent, values, value_tangent)

    left_1 = shifted(bundle, "z", 1)
    right_1 = shifted(bundle, "z", -1)
    slot_1 = shifted(qq, "x", -1)
    slot_3 = shifted(after(qq, slot_1), "x", 1)
    slot_2 = shifted(after(qq, slot_3), "x", 2)
    slots = [qq, slot_1, slot_2, slot_3]
    weight_left = shifted(out_weight, "y", 1)
    weight_right = shifted(out_weight, "y", -1)

    def run(key_blocks, kks, vvs, state, is_last=False):
        return attend(key_blocks, mask, block_frame, place, slots, kks, vvs, state, is_last)

    left_2 = shifted(left_1, "z", 1)
    right_2 = shifted(right_1, "z", -1)
    left_3 = shifted(left_2, "z", 1)
    right_3 = shifted(right_2, "z", -1)
    blocks = (bundle, left_1, right_1)
    state = run((0, -1, 1), blocks, blocks, None)

    weight_left, weight_right, _ = lax.optimization_barrier((weight_left, weight_right, state[1]))
    half = out_weight.shape[0] // 2
    far_a = shifted(weight_left[:half], "y", 1)
    far_b = shifted(weight_right[half:], "y", -1)

    held_left, held_right, _ = lax.optimization_barrier((left_3, right_3, state[1]))
    far_keys = shifted(held_left[:HEADS_HERE], "z", 1)
    far_values = shifted(held_right[HEADS_HERE:], "z", -1)
    blocks = (left_2, right_2, left_3, right_3)
    state = run((-2, 2, -3, 3), blocks, blocks, state)

    packed = run((4,), (far_keys,), (far_values,), state, is_last=True)
    packed, far_a, far_b = lax.optimization_barrier((packed, far_a, far_b))
    received = lax.all_to_all(
        packed.reshape(NX * NY, SLOT_TOK, PACKED), ("x", "y"), 0, 0, tiled=True
    )
    weights = (out_weight, weight_left, weight_right, far_a, far_b)
    main, tangent, other = project(place, received, weights)
    arrived = lax.ppermute(other, "c", [(0, 1), (1, 0)])
    return finish(main, tangent, arrived)


def solution(mesh):
    inner = Mesh(mesh.devices.reshape(NX, NZ, NY, NC), ("x", "z", "y", "c"))
    blk, head = ("x", "z"), ("y", "c")
    in_specs = (
        P(blk, head),
        P(blk, head),
        P(blk, head),
        P(blk, head),
        P(blk, head),
        P(blk, head),
        P(head, None, None),
        P(),
        P(head, None),
    )
    out_specs = (P(blk + head, None), P(blk + head, None))
    return jax.shard_map(body, mesh=inner, in_specs=in_specs, out_specs=out_specs, check_vma=False)
```

```python
import functools
import math

import jax
import jax.numpy as jnp
from jax import lax
from jax.experimental import pallas as pl
from jax.experimental.pallas import tpu as pltpu
from jax.sharding import Mesh
from jax.sharding import PartitionSpec as P

NX, NZ, NY, NC = 4, 8, 4, 2
HEADS_HERE = 3
HEAD_DIM = 128
PAIR = 2 * HEAD_DIM
TILE = 128
TOK = 256
TILES_HERE = TOK // TILE
FRAME_TILES = NX * NZ * TILES_HERE
WIDE = HEADS_HERE * PAIR
PACKED = WIDE + 128
PIECES = 3
WITH_ONES = HEAD_DIM + 16
SLOT_TOK = TOK // NY
DM = 3072
SCALING = HEAD_DIM ** (-0.5)
EXP_SCALE = SCALING * math.log2(math.e)
VERY_LOW = -1e30
VERY_HIGH = 1e30
VMEM_LIMIT = 56 * 1024 * 1024
NT = (((1,), (1,)), ((), ()))


def params():
    return pltpu.CompilerParams(vmem_limit_bytes=VMEM_LIMIT)


def prepare_kernel(q_ref, qt_ref, k_ref, kt_ref, v_ref, vt_ref, qq_ref, kv_ref):
    for h in range(HEADS_HERE):
        cols = pl.ds(h * HEAD_DIM, HEAD_DIM)
        qq_ref[:, pl.ds(h * PAIR, HEAD_DIM)] = qt_ref[:, cols]
        qq_ref[:, pl.ds(h * PAIR + HEAD_DIM, HEAD_DIM)] = q_ref[:, cols]
        kv_ref[h, :, 0:HEAD_DIM] = k_ref[:, cols]
        kv_ref[h, :, HEAD_DIM:PAIR] = kt_ref[:, cols]
        kv_ref[HEADS_HERE + h, 0:HEAD_DIM, :] = v_ref[:, cols].T
        kv_ref[HEADS_HERE + h, HEAD_DIM:PAIR, :] = vt_ref[:, cols].T


def prepare(queries, query_tangent, keys, key_tangent, values, value_tangent):
    return pl.pallas_call(
        prepare_kernel,
        out_shape=(
            jax.ShapeDtypeStruct((TOK, WIDE), jnp.bfloat16),
            jax.ShapeDtypeStruct((2 * HEADS_HERE, TOK, PAIR), jnp.bfloat16),
        ),
        compiler_params=params(),
        name="prepare",
    )(queries, query_tangent, keys, key_tangent, values, value_tangent)


def turned(array):
    size = array.shape[1]
    row = lax.broadcasted_iota(jnp.int32, (size, size), 0)
    col = lax.broadcasted_iota(jnp.int32, (size, size), 1)
    identity = jnp.where(row == col, 1.0, 0.0).astype(jnp.bfloat16)
    return lax.dot_general(identity, array, NT, preferred_element_type=jnp.float32).astype(jnp.bfloat16)


def products(kk, q2):
    s = lax.dot_general(
        kk[:, 0:HEAD_DIM], q2[:, HEAD_DIM:PAIR], NT, preferred_element_type=jnp.float32
    )
    return s, lax.dot_general(kk, q2, NT, preferred_element_type=jnp.float32)


def attend_slot(h, slot, key_blocks, s, t, mask_ref, frame_ref, place_ref, vv_ref, old):
    x, z = place_ref[0], place_ref[1]
    query_frame = frame_ref[((x + slot) & (NX - 1)) * NZ + z]
    lanes = lax.broadcasted_iota(jnp.int32, (1, TOK), 1)
    first = lanes < TILE
    m_old, l_old, d_old, acc_old = old
    lives = []
    m_new = m_old
    for at, offset in enumerate(key_blocks):
        key_frame = frame_ref[x * NZ + ((z + offset) & (NZ - 1))]
        for j in range(TILES_HERE):
            row = (h * FRAME_TILES + query_frame * TILES_HERE) * FRAME_TILES
            col = key_frame * TILES_HERE + j
            live = jnp.where(first, mask_ref[row + col], mask_ref[row + FRAME_TILES + col]) == 1
            tile = at * TILES_HERE + j
            top = jnp.max(s[tile * TILE : (tile + 1) * TILE], axis=0, keepdims=True) * EXP_SCALE
            m_new = jnp.maximum(m_new, jnp.where(live, top, VERY_LOW))
            lives.append(live)
    fade = jnp.exp2(m_old - m_new)
    weights, scaled = [], []
    for tile, live in enumerate(lives):
        rows = slice(tile * TILE, (tile + 1) * TILE)
        w = jnp.exp2(s[rows] * EXP_SCALE - jnp.where(live, m_new, VERY_HIGH))
        weights.append(w.astype(jnp.bfloat16))
        scaled.append((w * t[rows]).astype(jnp.bfloat16))
    o = jnp.dot(vv_ref[...], jnp.concatenate(weights, axis=0), preferred_element_type=jnp.float32)
    o2 = jnp.dot(
        vv_ref[0:WITH_ONES, :], jnp.concatenate(scaled, axis=0), preferred_element_type=jnp.float32
    )
    l_new = l_old * fade + o[HEAD_DIM : HEAD_DIM + 1]
    d_new = d_old * fade + SCALING * o2[HEAD_DIM : HEAD_DIM + 1]
    top = acc_old[0:HEAD_DIM] * fade + o[0:HEAD_DIM]
    bottom = acc_old[HEAD_DIM:PAIR] * fade + (o[WITH_ONES:] + SCALING * o2[0:HEAD_DIM])
    return m_new, l_new, d_new, top, bottom


def attend_kernel(key_blocks, is_first, is_last, *refs):
    count = len(key_blocks)
    mask_ref, frame_ref, place_ref = refs[:3]
    q_refs = refs[3 : 3 + NX]
    rest = refs[3 + NX :]
    kk_refs = [r.at[0] for r in rest[:count]]
    vv_refs = [r.at[0] for r in rest[count : 2 * count]]
    rest = rest[2 * count :]
    if not is_first:
        acc_in, stat_in = rest[:2]
        rest = rest[2:]
    rest, vv_ref = rest[:-1], rest[-1]
    h = pl.program_id(0)
    kk = jnp.concatenate([r[...] for r in kk_refs], axis=0)
    for at in range(count):
        cols = pl.ds(at * TOK, TOK)
        vv_ref[0:HEAD_DIM, cols] = vv_refs[at][0:HEAD_DIM, :]
        vv_ref[HEAD_DIM:WITH_ONES, cols] = jnp.ones((WITH_ONES - HEAD_DIM, TOK), jnp.bfloat16)
        vv_ref[WITH_ONES:, cols] = vv_refs[at][HEAD_DIM:PAIR, :]
    if is_last:
        side_ref = rest[1]

        @pl.when(h == 0)
        def _():
            side_ref[...] = jnp.zeros_like(side_ref)

    ahead = [products(kk, q_refs[slot][...]) for slot in range(NX)]
    for slot in range(NX):
        cols = pl.ds(slot * TOK, TOK)
        if is_first:
            zero = jnp.zeros((1, TOK), jnp.float32)
            old = (zero + VERY_LOW, zero, zero, jnp.zeros((PAIR, TOK), jnp.float32))
        else:
            old = (
                stat_in[0, 0:1, cols],
                stat_in[0, 1:2, cols],
                stat_in[0, 2:3, cols],
                acc_in[0, :, cols],
            )
        m, l, d, top, bottom = attend_slot(
            h, slot, key_blocks, *ahead[slot], mask_ref, frame_ref, place_ref, vv_ref, old
        )
        if not is_last:
            acc_out, stat_out = rest
            stat_out[0, 0:1, cols] = m
            stat_out[0, 1:2, cols] = l
            stat_out[0, 2:3, cols] = d
            acc_out[0, 0:HEAD_DIM, cols] = top
            acc_out[0, HEAD_DIM:PAIR, cols] = bottom
        else:
            out_ref = rest[0]
            some = l > 0.0
            inverse = jnp.where(some, 1.0 / jnp.where(some, l, 1.0), 0.0)
            level = jnp.where(some, m + jnp.log2(jnp.where(some, l, 1.0)), VERY_LOW)
            drift = d * inverse
            attn = top * inverse
            tangent = bottom * inverse - drift * attn
            target = (place_ref[0] + slot) & (NX - 1)
            columns = pl.multiple_of(h * PAIR, PAIR)
            both = jnp.concatenate((attn, tangent), axis=0).astype(jnp.bfloat16)
            out_ref[target, :, pl.ds(columns, PAIR)] = both.T
            for at, value in enumerate((level, drift)):
                left = value
                for p in range(PIECES):
                    piece = left.astype(jnp.bfloat16).astype(jnp.float32)
                    side_ref[slot, pl.ds(8 * p + HEADS_HERE * at + h, 1), :] = piece
                    left = left - piece

    if is_last:

        @pl.when(h == HEADS_HERE - 1)
        def _():
            for slot in range(NX):
                target = (place_ref[0] + slot) & (NX - 1)
                out_ref[target, :, pl.ds(WIDE, 128)] = side_ref[slot].astype(jnp.bfloat16).T


def attend(key_blocks, mask, frames, place, slots, kks, vvs, state, is_last):
    count = len(key_blocks)
    is_first = state is None
    smem = pl.BlockSpec(memory_space=pltpu.SMEM)
    acc_spec = pl.BlockSpec((1, PAIR, NX * TOK), lambda h: (h, 0, 0))
    stat_spec = pl.BlockSpec((1, 8, NX * TOK), lambda h: (h, 0, 0))
    in_specs = [smem] * 3
    in_specs += [pl.BlockSpec((TOK, PAIR), lambda h: (0, h))] * NX
    in_specs += [pl.BlockSpec((1, TOK, PAIR), lambda h: (h, 0, 0))] * count
    for vv in vvs:
        skip = vv.shape[0] - HEADS_HERE
        in_specs.append(pl.BlockSpec((1, PAIR, TOK), lambda h, skip=skip: (skip + h, 0, 0)))
    operands = [mask, frames, place, *slots, *kks, *vvs]
    if not is_first:
        in_specs += [acc_spec, stat_spec]
        operands += list(state)
    scratch = [pltpu.VMEM((WITH_ONES + HEAD_DIM, count * TOK), jnp.bfloat16)]
    if is_last:
        out_shape = jax.ShapeDtypeStruct((NX, TOK, PACKED), jnp.bfloat16)
        out_specs = pl.BlockSpec((NX, TOK, PACKED), lambda h: (0, 0, 0))
        scratch = [pltpu.VMEM((NX, 128, TOK), jnp.float32)] + scratch
    else:
        out_shape = (
            jax.ShapeDtypeStruct((HEADS_HERE, PAIR, NX * TOK), jnp.float32),
            jax.ShapeDtypeStruct((HEADS_HERE, 8, NX * TOK), jnp.float32),
        )
        out_specs = (acc_spec, stat_spec)
    return pl.pallas_call(
        functools.partial(attend_kernel, key_blocks, is_first, is_last),
        grid=(HEADS_HERE,),
        in_specs=in_specs,
        out_specs=out_specs,
        out_shape=out_shape,
        scratch_shapes=scratch,
        compiler_params=params(),
        cost_estimate=pl.CostEstimate(
            flops=count * NX * HEADS_HERE * 12 * TOK * TOK * HEAD_DIM,
            transcendentals=count * NX * HEADS_HERE * TOK * TOK,
            bytes_accessed=8 * 1024 * 1024,
        ),
        name="attend_last" if is_last else "attend",
    )(*operands)


COLS = 512


def project_kernel(place_ref, *refs):
    sources, (main_ref, tangent_ref, other_ref, mixed, r_ref, w_ref, sems) = refs[:6], refs[6:]
    copies = [pltpu.make_async_copy(sources[0], r_ref, sems.at[0])]
    start = 0
    for i, source in enumerate(sources[1:], 1):
        rows = pl.ds(start, source.shape[0])
        copies.append(pltpu.make_async_copy(source, w_ref.at[rows], sems.at[i]))
        start += source.shape[0]
    for copy in copies:
        copy.start()
    y, c = place_ref[2], place_ref[3]
    copies[0].wait()
    for rel, shift in enumerate((0, NY - 1, 1, 2)):
        group = (y + shift) & (NY - 1)
        sides = []
        for x in range(NX):
            side = r_ref[x * NY + group, :, pl.ds(WIDE, 128)].astype(jnp.float32)
            sides.append(side + (pltpu.roll(side, 128 - 8, 1) + pltpu.roll(side, 128 - 16, 1)))
        top = functools.reduce(jnp.maximum, sides)
        shares = [jnp.exp2(side - top) for side in sides]
        inverse = 1.0 / sum(shares)
        shares = [share * inverse for share in shares]
        drifts = [pltpu.roll(side, 128 - HEADS_HERE, 1) for side in sides]
        drift = sum(s * d for s, d in zip(shares, drifts))
        moves = [s * (d - drift) for s, d in zip(shares, drifts)]
        for h in range(HEADS_HERE):
            attn, tangent = 0.0, 0.0
            for x in range(NX):
                a = r_ref[x * NY + group, :, pl.ds(h * PAIR, HEAD_DIM)].astype(jnp.float32)
                t = r_ref[x * NY + group, :, pl.ds(h * PAIR + HEAD_DIM, HEAD_DIM)].astype(jnp.float32)
                share = shares[x][:, h : h + 1]
                attn = attn + share * a
                tangent = tangent + share * t + moves[x][:, h : h + 1] * a
            cols = pl.ds((rel * HEADS_HERE + h) * HEAD_DIM, HEAD_DIM)
            mixed[0:SLOT_TOK, cols] = attn.astype(jnp.bfloat16)
            mixed[SLOT_TOK : 2 * SLOT_TOK, cols] = tangent.astype(jnp.bfloat16)

    for copy in copies[1:]:
        copy.wait()
    half = SLOT_TOK // NC
    mine = c == 0
    for column in range(0, DM, COLS):
        cols = pl.ds(column, COLS)
        total = jnp.dot(mixed[...], w_ref[:, cols], preferred_element_type=jnp.float32)
        for which, own_ref in enumerate((main_ref, tangent_ref)):
            low = total[which * SLOT_TOK : which * SLOT_TOK + half]
            high = total[which * SLOT_TOK + half : (which + 1) * SLOT_TOK]
            own_ref[:, cols] = jnp.where(mine, low, high)
            other_ref[which, :, cols] = jnp.where(mine, high, low).astype(jnp.bfloat16)


def project(place, received, weights):
    half = SLOT_TOK // NC
    own_shape = jax.ShapeDtypeStruct((half, DM), jnp.float32)
    anywhere = pl.BlockSpec(memory_space=pltpu.HBM)
    operands = (received, *weights)
    return pl.pallas_call(
        project_kernel,
        in_specs=[pl.BlockSpec(memory_space=pltpu.SMEM)] + [anywhere] * len(operands),
        out_shape=(own_shape, own_shape, jax.ShapeDtypeStruct((2, half, DM), jnp.bfloat16)),
        scratch_shapes=[
            pltpu.VMEM((2 * SLOT_TOK, NY * HEADS_HERE * HEAD_DIM), jnp.bfloat16),
            pltpu.VMEM(received.shape, received.dtype),
            pltpu.VMEM((NY * HEADS_HERE * HEAD_DIM, DM), jnp.bfloat16),
            pltpu.SemaphoreType.DMA((len(operands),)),
        ],
        compiler_params=params(),
        name="project",
    )(place, *operands)


def shifted(block, axis, distance):
    size = lax.axis_size(axis)
    return lax.ppermute(block, axis, [(i, (i + distance) % size) for i in range(size)])


def after(array, *others):
    return lax.optimization_barrier((array, *others))[0]


def body(
    queries,
    keys,
    values,
    query_tangent,
    key_tangent,
    value_tangent,
    tile_mask,
    block_frame,
    out_weight,
):
    place = jnp.stack([lax.axis_index(a) for a in ("x", "z", "y", "c")]).astype(jnp.int32)
    mask = tile_mask.reshape(-1)
    qq, bundle = prepare(queries, query_tangent, keys, key_tangent, values, value_tangent)

    left_1 = shifted(bundle, "z", 1)
    right_1 = shifted(bundle, "z", -1)
    slot_1 = shifted(qq, "x", -1)
    slot_3 = shifted(after(qq, slot_1), "x", 1)
    slot_2 = shifted(after(qq, slot_3), "x", 2)
    slots = [qq, slot_1, slot_2, slot_3]
    weight_left = shifted(out_weight, "y", 1)
    weight_right = shifted(out_weight, "y", -1)

    def run(key_blocks, kks, vvs, state, is_last=False):
        return attend(key_blocks, mask, block_frame, place, slots, kks, vvs, state, is_last)

    left_2 = shifted(left_1, "z", 1)
    right_2 = shifted(right_1, "z", -1)
    left_3 = shifted(left_2, "z", 1)
    right_3 = shifted(right_2, "z", -1)
    blocks = (bundle, left_1, right_1)
    state = run((0, -1, 1), blocks, blocks, None)

    weight_left, weight_right, _ = lax.optimization_barrier((weight_left, weight_right, state[1]))
    half = out_weight.shape[0] // 2
    far_a = shifted(weight_left[:half], "y", 1)
    far_b = shifted(weight_right[half:], "y", -1)

    held_left, held_right, _ = lax.optimization_barrier((left_3, right_3, state[1]))
    far_keys = shifted(held_left[:HEADS_HERE], "z", 1)
    far_values = shifted(held_right[HEADS_HERE:], "z", -1)
    blocks = (left_2, right_2, left_3, right_3)
    state = run((-2, 2, -3, 3), blocks, blocks, state)

    packed = run((4,), (far_keys,), (far_values,), state, is_last=True)
    packed, far_a, far_b = lax.optimization_barrier((packed, far_a, far_b))
    received = lax.all_to_all(
        packed.reshape(NX * NY, SLOT_TOK, PACKED), ("x", "y"), 0, 0, tiled=True
    )
    weights = (out_weight, weight_left, weight_right, far_a, far_b)
    main, tangent, other = project(place, received, weights)
    arrived = lax.ppermute(other, "c", [(0, 1), (1, 0)])
    return tuple(
        (own + part.astype(jnp.float32)).astype(jnp.bfloat16)
        for own, part in ((main, arrived[0]), (tangent, arrived[1]))
    )


def solution(mesh):
    inner = Mesh(mesh.devices.reshape(NX, NZ, NY, NC), ("x", "z", "y", "c"))
    blk, head = ("x", "z"), ("y", "c")
    in_specs = (
        P(blk, head),
        P(blk, head),
        P(blk, head),
        P(blk, head),
        P(blk, head),
        P(blk, head),
        P(head, None, None),
        P(),
        P(head, None),
    )
    out_specs = (P(blk + head, None), P(blk + head, None))
    return jax.shard_map(body, mesh=inner, in_specs=in_specs, out_specs=out_specs, check_vma=False)
```

```python
import functools
import math

import jax
import jax.numpy as jnp
from jax import lax
from jax.experimental import pallas as pl
from jax.experimental.pallas import tpu as pltpu
from jax.sharding import Mesh
from jax.sharding import PartitionSpec as P

NX, NZ, NY, NC = 4, 8, 4, 2
HEADS_HERE = 3
HEAD_DIM = 128
PAIR = 2 * HEAD_DIM
TILE = 128
TOK = 256
TILES_HERE = TOK // TILE
FRAME_TILES = NX * NZ * TILES_HERE
WIDE = HEADS_HERE * PAIR
PACKED = WIDE + 128
PIECES = 3
WITH_ONES = HEAD_DIM + 16
SLOT_TOK = TOK // NY
DM = 3072
SCALING = HEAD_DIM ** (-0.5)
EXP_SCALE = SCALING * math.log2(math.e)
VERY_LOW = -1e30
VERY_HIGH = 1e30
VMEM_LIMIT = 56 * 1024 * 1024
NT = (((1,), (1,)), ((), ()))


def params():
    return pltpu.CompilerParams(vmem_limit_bytes=VMEM_LIMIT)


def prepare_kernel(q_ref, qt_ref, k_ref, kt_ref, v_ref, vt_ref, qq_ref, kv_ref):
    for h in range(HEADS_HERE):
        cols = pl.ds(h * HEAD_DIM, HEAD_DIM)
        qq_ref[:, pl.ds(h * PAIR, HEAD_DIM)] = qt_ref[:, cols]
        qq_ref[:, pl.ds(h * PAIR + HEAD_DIM, HEAD_DIM)] = q_ref[:, cols]
        kv_ref[h, :, 0:HEAD_DIM] = k_ref[:, cols]
        kv_ref[h, :, HEAD_DIM:PAIR] = kt_ref[:, cols]
        kv_ref[HEADS_HERE + h, 0:HEAD_DIM, :] = v_ref[:, cols].T
        kv_ref[HEADS_HERE + h, HEAD_DIM:PAIR, :] = vt_ref[:, cols].T


def prepare(queries, query_tangent, keys, key_tangent, values, value_tangent):
    return pl.pallas_call(
        prepare_kernel,
        out_shape=(
            jax.ShapeDtypeStruct((TOK, WIDE), jnp.bfloat16),
            jax.ShapeDtypeStruct((2 * HEADS_HERE, TOK, PAIR), jnp.bfloat16),
        ),
        compiler_params=params(),
        name="prepare",
    )(queries, query_tangent, keys, key_tangent, values, value_tangent)


def turned(array):
    size = array.shape[1]
    row = lax.broadcasted_iota(jnp.int32, (size, size), 0)
    col = lax.broadcasted_iota(jnp.int32, (size, size), 1)
    identity = jnp.where(row == col, 1.0, 0.0).astype(jnp.bfloat16)
    return lax.dot_general(identity, array, NT, preferred_element_type=jnp.float32).astype(jnp.bfloat16)


def products(kk, q2):
    s = lax.dot_general(
        kk[:, 0:HEAD_DIM], q2[:, HEAD_DIM:PAIR], NT, preferred_element_type=jnp.float32
    )
    return s, lax.dot_general(kk, q2, NT, preferred_element_type=jnp.float32)


def attend_slot(h, slot, key_blocks, s, t, mask_ref, frame_ref, place_ref, vv_ref, old):
    x, z = place_ref[0], place_ref[1]
    query_frame = frame_ref[((x + slot) & (NX - 1)) * NZ + z]
    lanes = lax.broadcasted_iota(jnp.int32, (1, TOK), 1)
    first = lanes < TILE
    m_old, l_old, d_old, acc_old = old
    lives = []
    m_new = m_old
    for at, offset in enumerate(key_blocks):
        key_frame = frame_ref[x * NZ + ((z + offset) & (NZ - 1))]
        for j in range(TILES_HERE):
            row = (h * FRAME_TILES + query_frame * TILES_HERE) * FRAME_TILES
            col = key_frame * TILES_HERE + j
            live = jnp.where(first, mask_ref[row + col], mask_ref[row + FRAME_TILES + col]) == 1
            tile = at * TILES_HERE + j
            top = jnp.max(s[tile * TILE : (tile + 1) * TILE], axis=0, keepdims=True) * EXP_SCALE
            m_new = jnp.maximum(m_new, jnp.where(live, top, VERY_LOW))
            lives.append(live)
    fade = jnp.exp2(m_old - m_new)
    weights, scaled = [], []
    for tile, live in enumerate(lives):
        rows = slice(tile * TILE, (tile + 1) * TILE)
        w = jnp.exp2(s[rows] * EXP_SCALE - jnp.where(live, m_new, VERY_HIGH))
        weights.append(w.astype(jnp.bfloat16))
        scaled.append((w * t[rows]).astype(jnp.bfloat16))
    o = jnp.dot(vv_ref[...], jnp.concatenate(weights, axis=0), preferred_element_type=jnp.float32)
    o2 = jnp.dot(
        vv_ref[0:WITH_ONES, :], jnp.concatenate(scaled, axis=0), preferred_element_type=jnp.float32
    )
    l_new = l_old * fade + o[HEAD_DIM : HEAD_DIM + 1]
    d_new = d_old * fade + SCALING * o2[HEAD_DIM : HEAD_DIM + 1]
    top = acc_old[0:HEAD_DIM] * fade + o[0:HEAD_DIM]
    bottom = acc_old[HEAD_DIM:PAIR] * fade + (o[WITH_ONES:] + SCALING * o2[0:HEAD_DIM])
    return m_new, l_new, d_new, top, bottom


def attend_kernel(key_blocks, is_first, is_last, *refs):
    count = len(key_blocks)
    mask_ref, frame_ref, place_ref = refs[:3]
    q_refs = refs[3 : 3 + NX]
    rest = refs[3 + NX :]
    kk_refs = [r.at[0] for r in rest[:count]]
    vv_refs = [r.at[0] for r in rest[count : 2 * count]]
    rest = rest[2 * count :]
    if not is_first:
        acc_in, stat_in = rest[:2]
        rest = rest[2:]
    rest, vv_ref = rest[:-1], rest[-1]
    h = pl.program_id(0)
    kk = jnp.concatenate([r[...] for r in kk_refs], axis=0)
    for at in range(count):
        cols = pl.ds(at * TOK, TOK)
        vv_ref[0:HEAD_DIM, cols] = vv_refs[at][0:HEAD_DIM, :]
        vv_ref[HEAD_DIM:WITH_ONES, cols] = jnp.ones((WITH_ONES - HEAD_DIM, TOK), jnp.bfloat16)
        vv_ref[WITH_ONES:, cols] = vv_refs[at][HEAD_DIM:PAIR, :]
    if is_last:
        side_ref = rest[1]

        @pl.when(h == 0)
        def _():
            side_ref[...] = jnp.zeros_like(side_ref)

    ahead = [products(kk, q_refs[slot][...]) for slot in range(NX)]
    for slot in range(NX):
        cols = pl.ds(slot * TOK, TOK)
        if is_first:
            zero = jnp.zeros((1, TOK), jnp.float32)
            old = (zero + VERY_LOW, zero, zero, jnp.zeros((PAIR, TOK), jnp.float32))
        else:
            old = (
                stat_in[0, 0:1, cols],
                stat_in[0, 1:2, cols],
                stat_in[0, 2:3, cols],
                acc_in[0, :, cols],
            )
        m, l, d, top, bottom = attend_slot(
            h, slot, key_blocks, *ahead[slot], mask_ref, frame_ref, place_ref, vv_ref, old
        )
        if not is_last:
            acc_out, stat_out = rest
            stat_out[0, 0:1, cols] = m
            stat_out[0, 1:2, cols] = l
            stat_out[0, 2:3, cols] = d
            acc_out[0, 0:HEAD_DIM, cols] = top
            acc_out[0, HEAD_DIM:PAIR, cols] = bottom
        else:
            out_ref = rest[0]
            some = l > 0.0
            inverse = jnp.where(some, 1.0 / jnp.where(some, l, 1.0), 0.0)
            level = jnp.where(some, m + jnp.log2(jnp.where(some, l, 1.0)), VERY_LOW)
            drift = d * inverse
            attn = top * inverse
            tangent = bottom * inverse - drift * attn
            target = (place_ref[0] + slot) & (NX - 1)
            columns = pl.multiple_of(h * PAIR, PAIR)
            both = jnp.concatenate((attn, tangent), axis=0).astype(jnp.bfloat16)
            out_ref[target, :, pl.ds(columns, PAIR)] = both.T
            for at, value in enumerate((level, drift)):
                left = value
                for p in range(PIECES):
                    piece = left.astype(jnp.bfloat16).astype(jnp.float32)
                    side_ref[slot, pl.ds(8 * p + HEADS_HERE * at + h, 1), :] = piece
                    left = left - piece

    if is_last:

        @pl.when(h == HEADS_HERE - 1)
        def _():
            for slot in range(NX):
                target = (place_ref[0] + slot) & (NX - 1)
                out_ref[target, :, pl.ds(WIDE, 128)] = side_ref[slot].astype(jnp.bfloat16).T


def attend(key_blocks, mask, frames, place, slots, kks, vvs, state, is_last):
    count = len(key_blocks)
    is_first = state is None
    smem = pl.BlockSpec(memory_space=pltpu.SMEM)
    acc_spec = pl.BlockSpec((1, PAIR, NX * TOK), lambda h: (h, 0, 0))
    stat_spec = pl.BlockSpec((1, 8, NX * TOK), lambda h: (h, 0, 0))
    in_specs = [smem] * 3
    in_specs += [pl.BlockSpec((TOK, PAIR), lambda h: (0, h))] * NX
    in_specs += [pl.BlockSpec((1, TOK, PAIR), lambda h: (h, 0, 0))] * count
    for vv in vvs:
        skip = vv.shape[0] - HEADS_HERE
        in_specs.append(pl.BlockSpec((1, PAIR, TOK), lambda h, skip=skip: (skip + h, 0, 0)))
    operands = [mask, frames, place, *slots, *kks, *vvs]
    if not is_first:
        in_specs += [acc_spec, stat_spec]
        operands += list(state)
    scratch = [pltpu.VMEM((WITH_ONES + HEAD_DIM, count * TOK), jnp.bfloat16)]
    if is_last:
        out_shape = jax.ShapeDtypeStruct((NX, TOK, PACKED), jnp.bfloat16)
        out_specs = pl.BlockSpec((NX, TOK, PACKED), lambda h: (0, 0, 0))
        scratch = [pltpu.VMEM((NX, 128, TOK), jnp.float32)] + scratch
    else:
        out_shape = (
            jax.ShapeDtypeStruct((HEADS_HERE, PAIR, NX * TOK), jnp.float32),
            jax.ShapeDtypeStruct((HEADS_HERE, 8, NX * TOK), jnp.float32),
        )
        out_specs = (acc_spec, stat_spec)
    return pl.pallas_call(
        functools.partial(attend_kernel, key_blocks, is_first, is_last),
        grid=(HEADS_HERE,),
        in_specs=in_specs,
        out_specs=out_specs,
        out_shape=out_shape,
        scratch_shapes=scratch,
        compiler_params=params(),
        cost_estimate=pl.CostEstimate(
            flops=count * NX * HEADS_HERE * 12 * TOK * TOK * HEAD_DIM,
            transcendentals=count * NX * HEADS_HERE * TOK * TOK,
            bytes_accessed=8 * 1024 * 1024,
        ),
        name="attend_last" if is_last else "attend",
    )(*operands)


COLS = 512
SPANS = 2


def project_kernel(place_ref, *refs):
    sources, (main_ref, tangent_ref, other_ref, mixed, r_ref, w_ref, sems) = refs[:6], refs[6:]
    first = pltpu.make_async_copy(sources[0], r_ref, sems.at[0, 0])
    first.start()
    spans = []
    for at in range(SPANS):
        cols = pl.ds(at * (DM // SPANS), DM // SPANS)
        start, copies = 0, []
        for i, source in enumerate(sources[1:], 1):
            rows = pl.ds(start, source.shape[0])
            copies.append(
                pltpu.make_async_copy(source.at[:, cols], w_ref.at[rows, cols], sems.at[i, at])
            )
            start += source.shape[0]
        for copy in copies:
            copy.start()
        spans.append(copies)
    y, c = place_ref[2], place_ref[3]
    first.wait()
    for rel, shift in enumerate((0, NY - 1, 1, 2)):
        group = (y + shift) & (NY - 1)
        sides = []
        for x in range(NX):
            side = r_ref[x * NY + group, :, pl.ds(WIDE, 128)].astype(jnp.float32)
            sides.append(side + (pltpu.roll(side, 128 - 8, 1) + pltpu.roll(side, 128 - 16, 1)))
        top = functools.reduce(jnp.maximum, sides)
        shares = [jnp.exp2(side - top) for side in sides]
        inverse = 1.0 / sum(shares)
        shares = [share * inverse for share in shares]
        drifts = [pltpu.roll(side, 128 - HEADS_HERE, 1) for side in sides]
        drift = sum(s * d for s, d in zip(shares, drifts))
        moves = [s * (d - drift) for s, d in zip(shares, drifts)]
        for h in range(HEADS_HERE):
            attn, tangent = 0.0, 0.0
            for x in range(NX):
                a = r_ref[x * NY + group, :, pl.ds(h * PAIR, HEAD_DIM)].astype(jnp.float32)
                t = r_ref[x * NY + group, :, pl.ds(h * PAIR + HEAD_DIM, HEAD_DIM)].astype(jnp.float32)
                share = shares[x][:, h : h + 1]
                attn = attn + share * a
                tangent = tangent + share * t + moves[x][:, h : h + 1] * a
            cols = pl.ds((rel * HEADS_HERE + h) * HEAD_DIM, HEAD_DIM)
            mixed[0:SLOT_TOK, cols] = attn.astype(jnp.bfloat16)
            mixed[SLOT_TOK : 2 * SLOT_TOK, cols] = tangent.astype(jnp.bfloat16)

    half = SLOT_TOK // NC
    mine = c == 0
    for column in range(0, DM, COLS):
        if column % (DM // SPANS) == 0:
            for copy in spans[column // (DM // SPANS)]:
                copy.wait()
        cols = pl.ds(column, COLS)
        total = jnp.dot(mixed[...], w_ref[:, cols], preferred_element_type=jnp.float32)
        for which, own_ref in enumerate((main_ref, tangent_ref)):
            low = total[which * SLOT_TOK : which * SLOT_TOK + half]
            high = total[which * SLOT_TOK + half : (which + 1) * SLOT_TOK]
            own_ref[:, cols] = jnp.where(mine, low, high)
            other_ref[which, :, cols] = jnp.where(mine, high, low).astype(jnp.bfloat16)


def project(place, received, weights):
    half = SLOT_TOK // NC
    own_shape = jax.ShapeDtypeStruct((half, DM), jnp.float32)
    anywhere = pl.BlockSpec(memory_space=pltpu.HBM)
    operands = (received, *weights)
    return pl.pallas_call(
        project_kernel,
        in_specs=[pl.BlockSpec(memory_space=pltpu.SMEM)] + [anywhere] * len(operands),
        out_shape=(own_shape, own_shape, jax.ShapeDtypeStruct((2, half, DM), jnp.bfloat16)),
        scratch_shapes=[
            pltpu.VMEM((2 * SLOT_TOK, NY * HEADS_HERE * HEAD_DIM), jnp.bfloat16),
            pltpu.VMEM(received.shape, received.dtype),
            pltpu.VMEM((NY * HEADS_HERE * HEAD_DIM, DM), jnp.bfloat16),
            pltpu.SemaphoreType.DMA((len(operands), SPANS)),
        ],
        compiler_params=params(),
        name="project",
    )(place, *operands)


def shifted(block, axis, distance):
    size = lax.axis_size(axis)
    return lax.ppermute(block, axis, [(i, (i + distance) % size) for i in range(size)])


def after(array, *others):
    return lax.optimization_barrier((array, *others))[0]


def body(
    queries,
    keys,
    values,
    query_tangent,
    key_tangent,
    value_tangent,
    tile_mask,
    block_frame,
    out_weight,
):
    place = jnp.stack([lax.axis_index(a) for a in ("x", "z", "y", "c")]).astype(jnp.int32)
    mask = tile_mask.reshape(-1)
    qq, bundle = prepare(queries, query_tangent, keys, key_tangent, values, value_tangent)

    left_1 = shifted(bundle, "z", 1)
    right_1 = shifted(bundle, "z", -1)
    slot_1 = shifted(qq, "x", -1)
    slot_3 = shifted(after(qq, slot_1), "x", 1)
    slot_2 = shifted(after(qq, slot_3), "x", 2)
    slots = [qq, slot_1, slot_2, slot_3]
    weight_left = shifted(out_weight, "y", 1)
    weight_right = shifted(out_weight, "y", -1)

    def run(key_blocks, kks, vvs, state, is_last=False):
        return attend(key_blocks, mask, block_frame, place, slots, kks, vvs, state, is_last)

    left_2 = shifted(left_1, "z", 1)
    right_2 = shifted(right_1, "z", -1)
    left_3 = shifted(left_2, "z", 1)
    right_3 = shifted(right_2, "z", -1)
    blocks = (bundle, left_1, right_1)
    state = run((0, -1, 1), blocks, blocks, None)

    weight_left, weight_right, _ = lax.optimization_barrier((weight_left, weight_right, state[1]))
    half = out_weight.shape[0] // 2
    far_a = shifted(weight_left[:half], "y", 1)
    far_b = shifted(weight_right[half:], "y", -1)

    held_left, held_right, _ = lax.optimization_barrier((left_3, right_3, state[1]))
    far_keys = shifted(held_left[:HEADS_HERE], "z", 1)
    far_values = shifted(held_right[HEADS_HERE:], "z", -1)
    blocks = (left_2, right_2, left_3, right_3)
    state = run((-2, 2, -3, 3), blocks, blocks, state)

    packed = run((4,), (far_keys,), (far_values,), state, is_last=True)
    packed, far_a, far_b = lax.optimization_barrier((packed, far_a, far_b))
    received = lax.all_to_all(
        packed.reshape(NX * NY, SLOT_TOK, PACKED), ("x", "y"), 0, 0, tiled=True
    )
    weights = (out_weight, weight_left, weight_right, far_a, far_b)
    main, tangent, other = project(place, received, weights)
    arrived = lax.ppermute(other, "c", [(0, 1), (1, 0)])
    return tuple(
        (own + part.astype(jnp.float32)).astype(jnp.bfloat16)
        for own, part in ((main, arrived[0]), (tangent, arrived[1]))
    )


def solution(mesh):
    inner = Mesh(mesh.devices.reshape(NX, NZ, NY, NC), ("x", "z", "y", "c"))
    blk, head = ("x", "z"), ("y", "c")
    in_specs = (
        P(blk, head),
        P(blk, head),
        P(blk, head),
        P(blk, head),
        P(blk, head),
        P(blk, head),
        P(head, None, None),
        P(),
        P(head, None),
    )
    out_specs = (P(blk + head, None), P(blk + head, None))
    return jax.shard_map(body, mesh=inner, in_specs=in_specs, out_specs=out_specs, check_vma=False)
```
